768 devices in a mesh: dom: 16 (over x, z_lo), grp: 48 (over z_hi, y, core).
Axes of the slice: x: 4, y: 8, z: 12 (z_hi: 3, z_lo: 4; z = z_hi * 4 + z_lo), core: 2. Of those that a mesh axis runs over, the one named last changes fastest.
Arguments:
- features: float32 [196608, 768], P(('dom', 'grp')), may hold values from -6 to 6
- factor: float32 [768, 768], P(None, 'grp'), as said below
- slab_map: int32 [196608], P('dom'), may hold values from 0 to 12287, as said below
- kinds: int32 [192, 8, 128], P('dom'), may hold values from 0 to 7
- kind_table: float32 [8, 27], replicated, may hold values from -0.15 to 0.15
Outputs:
- filtered: float32 [768, 192, 8, 128], P('grp', 'dom')
The draws below stay inside these ranges and needn't reach their ends.
Inputs may be any that keep to these rules, and one draw needn't show every extreme that they name: `slab_map`: each aligned block of 12288 entries (one slab) is a permutation of 0 to 12287. `factor`: upper triangular with diagonal between 0.5 and 1.5.
All inputs are finite; a program needn't handle non-finite values.
Results may differ from the reference program's by a relative error of at most 0.00009.
Values sent between devices are 32-bit elements; how exact they have to be, the bound alone decides.
A program may use at most 64 MiB of HBM per device.

```python
import jax
import jax.numpy as jnp
from jax import lax

STATES = 768
PY = 8
PZ = 128
KINDS = 8
CHEB = 4
SLAB = 12288
NX = 192
NODES = 196608


def draw_factor(key, part):
    base = jax.random.fold_in(key, 11)
    key_upper, key_diag = jax.random.split(base)
    upper = jax.random.normal(key_upper, (STATES, STATES), jnp.float32)
    diagonal = jax.random.uniform(key_diag, (STATES,), jnp.float32, 0.5, 1.5)
    scaled = jnp.triu(upper * (0.5 / jnp.sqrt(jnp.float32(STATES))), 1)
    return scaled + jnp.diag(diagonal)


def draw_slab_map(key, part):
    base = jax.random.fold_in(key, 23)
    slab_keys = jax.random.split(base, NODES // SLAB)
    orders = jax.vmap(lambda single: jax.random.permutation(single, SLAB))(slab_keys)
    return orders.reshape(NODES).astype(jnp.int32)


def set_ends(drawn, rng, low, largest):
    spot = [jax.random.randint(jax.random.fold_in(rng, axis), (), 0, length) for axis, length in enumerate(drawn.shape)]
    widest = drawn.shape.index(max(drawn.shape))
    next_to = spot[:widest] + [(spot[widest] + 1) % drawn.shape[widest]] + spot[widest + 1:]
    return drawn.at[tuple(spot)].set(low).at[tuple(next_to)].set(largest)


def steps_of(key, extent, cuts, smallest, top_value):
    level, own = 1.0, jax.random.fold_in(key, 6)
    for axis_at, blocks in cuts:
        draws = jnp.exp(jax.random.uniform(jax.random.fold_in(own, axis_at), (blocks,), jnp.float32, smallest / len(cuts), top_value / len(cuts)))
        level = level * jnp.repeat(draws, extent[axis_at] // blocks).reshape([-1 if axis == axis_at else 1 for axis in range(len(extent))])
    return level


def scatter_about(rng, shape, scale, bound, pieces=(), held_as=jnp.bfloat16):
    entries = jax.random.normal(rng, shape, jnp.float32) * scale
    if len(pieces) > 0:
        entries = steps_of(rng, shape, pieces, -0.22, 0.18) * entries
    return jnp.clip(entries, min=-bound, max=bound).astype(held_as)


def setup_inputs(seed: int = 0) -> dict:
    key_list = jax.random.split(jax.random.key(seed), 6)
    features = scatter_about(key_list[0], (NODES, STATES), 1.0, 6.0, ((0, 768),), jnp.float32)
    factor = draw_factor(jax.random.fold_in(key_list[5], 71), 0)
    slab_map = draw_slab_map(jax.random.fold_in(key_list[5], 71), 0)
    kinds = set_ends(jax.random.randint(key_list[3], (NX, PY, PZ), 0, KINDS), jax.random.fold_in(key_list[3], 1), 0, KINDS - 1).astype(jnp.int32)
    kind_table = jnp.clip(jax.random.uniform(key_list[4], (KINDS, 27), jnp.float32, -0.15, 0.15), -0.15, 0.15)
    return {"features": features, "factor": factor, "slab_map": slab_map, "kinds": kinds, "kind_table": kind_table}


def stencil_apply(values, coeffs):
    extent_x, extent_y, extent_z = values.shape[1], values.shape[2], values.shape[3]
    padded = jnp.pad(values, ((0, 0), (1, 1), (1, 1), (1, 1)))
    summed = jnp.zeros(values.shape, jnp.float32)
    for shift_x in (-1, 0, 1):
        for shift_y in (-1, 0, 1):
            for shift_z in (-1, 0, 1):
                offset = (shift_x + 1) * 9 + (shift_y + 1) * 3 + (shift_z + 1)
                window = padded[:, 1 + shift_x:1 + shift_x + extent_x, 1 + shift_y:1 + shift_y + extent_y, 1 + shift_z:1 + shift_z + extent_z]
                summed = summed + coeffs[offset][None] * window
    return summed


def reference(features, factor, slab_map, kinds, kind_table):
    rotated = jnp.dot(features, factor, preferred_element_type=jnp.float32, precision=lax.Precision.HIGHEST)
    owner = (jnp.arange(NODES, dtype=jnp.int32) // SLAB) * SLAB + slab_map.astype(jnp.int32)
    placed = jnp.zeros((NODES, STATES), jnp.float32).at[owner].set(rotated)
    lattice = placed.T.reshape(STATES // 16, 16, NX, PY, PZ)
    coeffs = jnp.moveaxis(kind_table[kinds], -1, 0)

    def filter_block(block):
        earlier = block
        current = stencil_apply(block, coeffs)
        for degree in range(1, CHEB):
            following = 2.0 * stencil_apply(current, coeffs) - earlier
            earlier = current
            current = following
        return current

    result = lax.map(filter_block, lattice)
    return result.reshape(STATES, NX, PY, PZ)
```

```python
import functools

import jax
import jax.numpy as jnp
from jax import lax
from jax.experimental import pallas as pl
from jax.experimental.pallas import tpu as pltpu
from jax.sharding import PartitionSpec as P

CHEB = 4
NH = 3
MESH = pl.DeviceIdType.MESH
F32 = jnp.float32
BF16 = jnp.bfloat16


def split(value):
    high = value.astype(BF16)
    low = (value - high.astype(F32)).astype(BF16)
    return high, low


def nt_dot(a, b):
    return lax.dot_general(a, b, (((1,), (1,)), ((), ())), preferred_element_type=F32)


def kernel(
    doms,
    ny,
    feat_ref,
    fac_ref,
    map_ref,
    kinds_ref,
    table_ref,
    out_ref,
    fac_all,
    fcat,
    rot,
    moved,
    acc,
    coef,
    terms,
    z_send,
    z_recv,
    y_send,
    y_recv,
    p_send,
    p_recv,
    a_send,
    a_recv,
    h_send,
    h_recv,
):
    peers = NH * ny * 2
    half = ny // 2
    sb, states = fac_ref.shape
    nb = feat_ref.shape[0]
    kw = states // NH
    planes = kinds_ref.shape[0]
    rows = map_ref.shape[0] * nb // 256

    d = lax.axis_index("dom")
    g = lax.axis_index("grp")
    h = g // (2 * ny)
    y = lax.rem(g // 2, ny)
    c = lax.rem(g, 2)

    def pid(hh, yy, cc):
        return (hh * ny + yy) * 2 + cc

    def wrap(yy):
        return lax.rem(yy + 2 * ny, ny)

    barrier = pltpu.get_barrier_semaphore()

    def greet(i, carry):
        pl.semaphore_signal(barrier, inc=1, device_id=(d, lax.rem(g + i, peers)), device_id_type=MESH)
        return carry

    lax.fori_loop(1, peers, greet, 0)

    @pl.when(d > 0)
    def _():
        pl.semaphore_signal(barrier, inc=1, device_id=(d - 1, g), device_id_type=MESH)

    @pl.when(d < doms - 1)
    def _():
        pl.semaphore_signal(barrier, inc=1, device_id=(d + 1, g), device_id_type=MESH)

    own_rows = pl.ds(pl.multiple_of(g * sb, sb), sb)
    fac_all[own_rows, :] = fac_ref[...]
    f_high, f_low = split(feat_ref[...])
    for t in range(NH):
        part = slice(t * kw, (t + 1) * kw)
        fcat[t, :, 0:kw] = f_high[:, part]
        fcat[t, :, kw : 2 * kw] = f_low[:, part]
        fcat[t, :, 2 * kw : 3 * kw] = f_high[:, part]

    expected = peers - 1 + (d > 0).astype(jnp.int32) + (d < doms - 1).astype(jnp.int32)
    pl.semaphore_wait(barrier, expected)

    def block(hh, yy, cc):
        row = pl.multiple_of(pid(hh, yy, cc) * sb, sb)
        return fac_all.at[pl.ds(row, sb), pl.ds(0, kw * (hh + 1))]

    def z_copy(hs, step):
        to = lax.rem(h + step, NH)
        return pltpu.make_async_remote_copy(
            src_ref=block(hs, y, c),
            dst_ref=block(hs, y, c),
            send_sem=z_send.at[step - 1],
            recv_sem=z_recv.at[hs],
            device_id=(d, pid(to, y, c)),
            device_id_type=MESH,
        )

    def y_copy(slot, hh, from_y, to_y):
        return pltpu.make_async_remote_copy(
            src_ref=block(hh, from_y, c),
            dst_ref=block(hh, from_y, c),
            send_sem=y_send.at[slot, hh],
            recv_sem=y_recv.at[slot, hh],
            device_id=(d, pid(h, to_y, c)),
            device_id_type=MESH,
        )

    def p_copy(slot, hh, yy, cc):
        return pltpu.make_async_remote_copy(
            src_ref=block(hh, yy, cc),
            dst_ref=block(hh, yy, cc),
            send_sem=p_send.at[slot, hh],
            recv_sem=p_recv.at[slot, hh],
            device_id=(d, pid(h, y, 1 - c)),
            device_id_type=MESH,
        )

    right, left = wrap(y + 1), wrap(y - 1)
    last = 2 * half - 1
    last_from = wrap(jnp.where(c == 0, y - (half - 1), y + (half - 1)))
    last_to = jnp.where(c == 0, right, left)

    def slot_y(slot):
        if slot == 0:
            return y
        t = (slot + 1) // 2
        if slot == last:
            return wrap(y + half)
        return wrap(y - t) if slot % 2 == 1 else wrap(y + t)

    for hs in range(NH):

        @pl.when(h == hs)
        def _(hs=hs):
            for step in range(1, NH):
                z_copy(hs, step).start()
            y_copy(1, hs, y, right).start()
            if last != 1:
                y_copy(2, hs, y, left).start()
            p_copy(0, hs, y, c).start()

    for hs in range(NH):

        @pl.when(h != hs)
        def _(hs=hs):
            z_copy(hs, 1).wait_recv()
            y_copy(1, hs, y, right).start()
            if last != 1:
                y_copy(2, hs, y, left).start()
            p_copy(0, hs, y, c).start()

    def a_copy(hh, yy, cc):
        to = pid(hh, yy, cc)
        return pltpu.make_async_remote_copy(
            src_ref=rot.at[to],
            dst_ref=moved.at[g],
            send_sem=a_send.at[to],
            recv_sem=a_recv.at[g],
            device_id=(d, to),
            device_id_type=MESH,
        )

    def rotate(slot):
        yy = slot_y(slot)
        for hh in range(NH):
            p_copy(slot, hh, yy, 1 - c).wait_recv()
        pair = [fac_all[pl.ds(pl.multiple_of(pid(hh, yy, 0) * sb, 2 * sb), 2 * sb), 0 : kw * (hh + 1)] for hh in range(NH)]
        totals = [None] * NH
        for t in range(NH):
            stacked = jnp.concatenate([pair[hh][:, t * kw : (t + 1) * kw] for hh in range(t, NH)], axis=0)
            high, low = split(stacked)
            product = nt_dot(jnp.concatenate([high, high, low], axis=1), fcat[t])
            for hh in range(t, NH):
                piece = product[(hh - t) * 2 * sb : (hh - t + 1) * 2 * sb]
                totals[hh] = piece if totals[hh] is None else totals[hh] + piece
        for hh in range(NH):
            for cc in range(2):
                rot[pid(hh, yy, cc)] = totals[hh][cc * sb : (cc + 1) * sb]
        for step in range(1, NH + 1):
            for cs in range(2):
                hh = lax.rem(h + step, NH)
                cc = lax.rem(c + 1 + cs, 2)
                if slot == 0 and step == NH and cs == 1:
                    moved[g] = rot[g]
                else:
                    a_copy(hh, yy, cc).start()

    rotate(0)
    for t in range(1, half + 1):
        slots = [last] if t == half else [2 * t - 1, 2 * t]
        for hh in range(NH):
            for slot in slots:
                yy = slot_y(slot)
                y_copy(slot, hh, yy, right).wait_recv()
                if t < half - 1:
                    y_copy(slot + 2, hh, yy, right if slot % 2 == 1 else left).start()
                p_copy(slot, hh, yy, c).start()
            if t == half - 1:
                y_copy(last, hh, last_from, last_to).start()
        for slot in slots:
            rotate(slot)

    lane = lax.broadcasted_iota(jnp.int32, kinds_ref.shape[1:], 1)
    sub = lax.broadcasted_iota(jnp.int32, kinds_ref.shape[1:], 0)
    py, pz = kinds_ref.shape[1], kinds_ref.shape[2]

    def coefficients(x, carry):
        for dz in (-1, 0, 1):
            kr = kinds_ref[x]
            if dz != 0:
                kr = pltpu.roll(kr, dz % pz, 1)
            hits = [kr == j for j in range(table_ref.shape[0])]
            for dx in (-1, 0, 1):
                for dy in (-1, 0, 1):
                    o = (dx + 1) * 9 + (dy + 1) * 3 + dz + 1
                    value = jnp.zeros(kr.shape, F32)
                    for j in range(table_ref.shape[0]):
                        value = jnp.where(hits[j], 2.0 * table_ref[j, o], value)
                    if dz == 1:
                        value = jnp.where(lane == 0, 0.0, value)
                    if dz == -1:
                        value = jnp.where(lane == pz - 1, 0.0, value)
                    if dy == 1:
                        value = jnp.where(sub == py - 1, 0.0, value)
                    if dy == -1:
                        value = jnp.where(sub == 0, 0.0, value)
                    coef[x, o] = value
        return carry

    lax.fori_loop(0, planes, coefficients, 0)
    acc[...] = jnp.zeros_like(acc)

    def place(i, carry):
        hh = lax.rem(i, NH)
        slot = i // NH
        t = (slot + 1) // 2
        yy = wrap(jnp.where(lax.rem(slot, 2) == 1, y + t, y - t))
        a_parts, b_parts = [], []
        for cc in range(2):
            src = pid(hh, yy, cc)

            @pl.when(src != g)
            def _(src=src):
                pltpu.make_async_remote_copy(
                    src_ref=rot.at[src],
                    dst_ref=moved.at[src],
                    send_sem=a_send.at[src],
                    recv_sem=a_recv.at[src],
                    device_id=(d, src),
                    device_id_type=MESH,
                ).wait_recv()

            cell = map_ref[pl.ds(src, 1), :]
            row = (cell // 2048) * 8 + lax.rem(cell // 128, 8)
            column = lax.rem(cell // 1024, 2) * 128 + lax.rem(cell, 128)
            high, low = split(moved[src])
            row16 = jnp.broadcast_to(row.astype(F32), (sb, nb)).astype(BF16)
            for value in (high, low):
                a_parts.append(
                    jnp.concatenate([jnp.where(row16 == BF16(r), value, BF16(0)) for r in range(rows)], axis=0)
                )
            wide = jnp.broadcast_to(column, (256, nb))
            onehot = (wide == lax.broadcasted_iota(jnp.int32, (256, nb), 0)).astype(F32).astype(BF16)
            b_parts += [onehot, onehot]
        product = nt_dot(jnp.concatenate(a_parts, axis=1), jnp.concatenate(b_parts, axis=1))
        acc[0] += product[:, 0:128]
        acc[1] += product[:, 128:256]
        return carry

    lax.fori_loop(0, NH * ny, place, 0)

    def lift(x):
        def one(s, carry):
            terms[0, x + 1, s] = acc[x % 2 if isinstance(x, int) else 0, pl.ds((x // 2) * 8 * sb + s, 8, stride=sb), :]
            return carry

        lax.fori_loop(0, sb, one, 0, unroll=4)

    def halo(k, up):
        to = d + 1 if up else d - 1
        return pltpu.make_async_remote_copy(
            src_ref=terms.at[k, planes if up else 1],
            dst_ref=terms.at[k, 0 if up else planes + 1],
            send_sem=h_send.at[k, 0 if up else 1],
            recv_sem=h_recv.at[k, 0 if up else 1],
            device_id=(to, g),
            device_id_type=MESH,
        )

    def send_edges(k):
        @pl.when(d < doms - 1)
        def _():
            halo(k, True).start()

        @pl.when(d > 0)
        def _():
            halo(k, False).start()

    def wait_edges(k):
        @pl.when(d > 0)
        def _():
            halo(k, True).wait_recv()

        @pl.when(d < doms - 1)
        def _():
            halo(k, False).wait_recv()

    @pl.when(d == 0)
    def _():
        for k in range(CHEB):
            terms[k, 0] = jnp.zeros(terms.shape[2:], F32)

    @pl.when(d == doms - 1)
    def _():
        for k in range(CHEB):
            terms[k, planes + 1] = jnp.zeros(terms.shape[2:], F32)

    lift(0)
    lift(planes - 1)
    send_edges(0)
    for x in range(1, planes - 1):
        lift(x)

    def plane(k, x):
        cs = [coef[x, o] for o in range(27)]

        def one(s, carry):
            sums = [None, None, None]
            for dx in range(3):
                mid = terms[k, x + dx, s]
                shifted = (pltpu.roll(mid, 1, 0), mid, pltpu.roll(mid, py - 1, 0))
                for dy in range(3):
                    for dz in range(3):
                        term = cs[dx * 9 + dy * 3 + dz] * shifted[dy]
                        sums[dz] = term if sums[dz] is None else sums[dz] + term
            total = sums[1] + pltpu.roll(sums[0], 1, 1) + pltpu.roll(sums[2], pz - 1, 1)
            if k == 0:
                total = 0.5 * total
            else:
                total = total - terms[k - 1, x + 1, s]
            if k == CHEB - 1:
                out_ref[s, x] = total
            else:
                terms[k + 1, x + 1, s] = total
            return carry

        lax.fori_loop(0, sb, one, 0, unroll=4)

    for k in range(CHEB):

        def interior(x, carry, k=k):
            plane(k, x)
            return carry

        lax.fori_loop(1, planes - 1, interior, 0)
        wait_edges(k)
        plane(k, 0)
        plane(k, planes - 1)
        if k < CHEB - 1:
            send_edges(k + 1)

    for step in range(1, NH):
        for hs in range(NH):

            @pl.when(h == hs)
            def _(hs=hs, step=step):
                z_copy(hs, step).wait_send()

    for slot in range(1, 2 * half):
        for hh in range(NH):
            y_copy(slot, hh, y, right).wait_send()
    for slot in range(2 * half):
        for hh in range(NH):
            p_copy(slot, hh, y, c).wait_send()

    def sent(i, carry):
        to = lax.rem(g + i, peers)
        pltpu.make_async_remote_copy(
            src_ref=rot.at[to],
            dst_ref=moved.at[g],
            send_sem=a_send.at[to],
            recv_sem=a_recv.at[g],
            device_id=(d, to),
            device_id_type=MESH,
        ).wait_send()
        return carry

    lax.fori_loop(1, peers, sent, 0)
    for k in range(CHEB):

        @pl.when(d < doms - 1)
        def _(k=k):
            halo(k, True).wait_send()

        @pl.when(d > 0)
        def _(k=k):
            halo(k, False).wait_send()


def local(doms, peers, features, factor, slab_map, kinds, kind_table):
    nb, states = features.shape
    sb = factor.shape[1]
    ny = peers // (2 * NH)
    planes, py, pz = kinds.shape
    cells = slab_map.shape[0]
    dma = pltpu.SemaphoreType.DMA
    vmem = pl.BlockSpec(memory_space=pltpu.VMEM)
    return pl.pallas_call(
        functools.partial(kernel, doms, ny),
        out_shape=jax.ShapeDtypeStruct((sb, planes, py, pz), F32),
        in_specs=[vmem, vmem, vmem, vmem, pl.BlockSpec(memory_space=pltpu.SMEM)],
        out_specs=vmem,
        scratch_shapes=[
            pltpu.VMEM((states, states), F32),
            pltpu.VMEM((NH, nb, states), BF16),
            pltpu.VMEM((peers, sb, nb), F32),
            pltpu.VMEM((peers, sb, nb), F32),
            pltpu.VMEM((2, cells // 256 * sb, 128), F32),
            pltpu.VMEM((planes, 27, py, pz), F32),
            pltpu.VMEM((CHEB, planes + 2, sb, py, pz), F32),
            dma((NH - 1,)),
            dma((NH,)),
            dma((ny, NH)),
            dma((ny, NH)),
            dma((ny, NH)),
            dma((ny, NH)),
            dma((peers,)),
            dma((peers,)),
            dma((CHEB, 2)),
            dma((CHEB, 2)),
        ],
        compiler_params=pltpu.CompilerParams(
            collective_id=0, has_side_effects=True, vmem_limit_bytes=48 * 1024 * 1024
        ),
    )(features, factor.T, slab_map.reshape(peers, nb), kinds, kind_table)


def solution(mesh):
    return jax.shard_map(
        functools.partial(local, mesh.shape["dom"], mesh.shape["grp"]),
        mesh=mesh,
        in_specs=(P(("dom", "grp"), None), P(None, "grp"), P("dom"), P("dom", None, None), P()),
        out_specs=P("grp", "dom", None, None),
        check_vma=False,
    )
```

```python
import functools

import jax
import jax.numpy as jnp
from jax import lax
from jax.experimental import pallas as pl
from jax.experimental.pallas import tpu as pltpu
from jax.sharding import PartitionSpec as P

CHEB = 4
NH = 3
DEEP = CHEB - 1
LAG = 2
MESH = pl.DeviceIdType.MESH
F32 = jnp.float32
BF16 = jnp.bfloat16


def split(value):
    high = value.astype(BF16)
    low = (value - high.astype(F32)).astype(BF16)
    return high, low


def nt_dot(a, b):
    return lax.dot_general(a, b, (((1,), (1,)), ((), ())), preferred_element_type=F32)


def kernel(
    doms,
    ny,
    feat_hbm,
    fac_hbm,
    map_hbm,
    kinds_hbm,
    table_ref,
    out_ref,
    feat_ref,
    map_ref,
    kinds_ref,
    fac_all,
    fcat,
    rot,
    moved,
    acc,
    coef,
    terms,
    z_send,
    z_recv,
    y_send,
    y_recv,
    p_send,
    p_recv,
    a_send,
    a_recv,
    h_send,
    h_recv,
    k_send,
    k_recv,
    fetched,
):
    peers = NH * ny * 2
    half = ny // 2
    sb, states = fac_hbm.shape
    nb = feat_hbm.shape[0]
    kw = states // NH
    planes = kinds_hbm.shape[0]
    rows = map_hbm.shape[0] * map_hbm.shape[1] // 256

    d = lax.axis_index("dom")
    g = lax.axis_index("grp")
    h = g // (2 * ny)
    y = lax.rem(g // 2, ny)
    c = lax.rem(g, 2)

    def pid(hh, yy, cc):
        return (hh * ny + yy) * 2 + cc

    def wrap(yy):
        return lax.rem(yy + 2 * ny, ny)

    own_rows = pl.ds(pl.multiple_of(g * sb, sb), sb)
    fetches = [
        pltpu.make_async_copy(fac_hbm, fac_all.at[own_rows], fetched.at[0]),
        pltpu.make_async_copy(feat_hbm, feat_ref, fetched.at[1]),
        pltpu.make_async_copy(kinds_hbm, kinds_ref.at[pl.ds(DEEP, planes)], fetched.at[2]),
        pltpu.make_async_copy(map_hbm, map_ref, fetched.at[3]),
    ]
    for fetch in fetches:
        fetch.start()

    barrier = pltpu.get_barrier_semaphore()
    near = [pid(h, wrap(y + 1), c), pid(h, wrap(y - 1), c), pid(h, y, 1 - c)]
    near += [pid(lax.rem(h + step, NH), y, c) for step in range(1, NH)]
    for to in near:
        pl.semaphore_signal(barrier, inc=1, device_id=(d, to), device_id_type=MESH)

    @pl.when(d > 0)
    def _():
        pl.semaphore_signal(barrier, inc=1, device_id=(d - 1, g), device_id_type=MESH)

    @pl.when(d < doms - 1)
    def _():
        pl.semaphore_signal(barrier, inc=1, device_id=(d + 1, g), device_id_type=MESH)

    for fetch in fetches:
        fetch.wait()
    f_high, f_low = split(feat_ref[...])
    for t in range(NH):
        part = slice(t * kw, (t + 1) * kw)
        fcat[t, :, 0:kw] = f_high[:, part]
        fcat[t, :, kw : 2 * kw] = f_low[:, part]
        fcat[t, :, 2 * kw : 3 * kw] = f_high[:, part]

    expected = len(near) + (d > 0).astype(jnp.int32) + (d < doms - 1).astype(jnp.int32)
    pl.semaphore_wait(barrier, expected)

    def block(hh, yy, cc):
        row = pl.multiple_of(pid(hh, yy, cc) * sb, sb)
        return fac_all.at[pl.ds(row, sb), pl.ds(0, kw * (hh + 1))]

    def z_copy(hs, step):
        to = lax.rem(h + step, NH)
        return pltpu.make_async_remote_copy(
            src_ref=block(hs, y, c),
            dst_ref=block(hs, y, c),
            send_sem=z_send.at[step - 1],
            recv_sem=z_recv.at[hs],
            device_id=(d, pid(to, y, c)),
            device_id_type=MESH,
        )

    def y_copy(slot, hh, from_y, to_y):
        return pltpu.make_async_remote_copy(
            src_ref=block(hh, from_y, c),
            dst_ref=block(hh, from_y, c),
            send_sem=y_send.at[slot, hh],
            recv_sem=y_recv.at[slot, hh],
            device_id=(d, pid(h, to_y, c)),
            device_id_type=MESH,
        )

    def p_copy(slot, hh, yy, cc):
        return pltpu.make_async_remote_copy(
            src_ref=block(hh, yy, cc),
            dst_ref=block(hh, yy, cc),
            send_sem=p_send.at[slot, hh],
            recv_sem=p_recv.at[slot, hh],
            device_id=(d, pid(h, y, 1 - c)),
            device_id_type=MESH,
        )

    right, left = wrap(y + 1), wrap(y - 1)
    last = 2 * half - 1
    last_from = wrap(jnp.where(c == 0, y - (half - 1), y + (half - 1)))
    last_to = jnp.where(c == 0, right, left)

    def slot_y(slot):
        if slot == 0:
            return y
        t = (slot + 1) // 2
        if slot == last:
            return wrap(y + half)
        return wrap(y - t) if slot % 2 == 1 else wrap(y + t)

    for hs in range(NH):

        @pl.when(h == hs)
        def _(hs=hs):
            for step in range(1, NH):
                z_copy(hs, step).start()
            y_copy(1, hs, y, right).start()
            if last != 1:
                y_copy(2, hs, y, left).start()
            p_copy(0, hs, y, c).start()

    for hs in range(NH):

        @pl.when(h != hs)
        def _(hs=hs):
            z_copy(hs, 1).wait_recv()
            y_copy(1, hs, y, right).start()
            if last != 1:
                y_copy(2, hs, y, left).start()
            p_copy(0, hs, y, c).start()

    def a_copy(hh, yy, cc):
        to = pid(hh, yy, cc)
        return pltpu.make_async_remote_copy(
            src_ref=rot.at[to],
            dst_ref=moved.at[g],
            send_sem=a_send.at[to],
            recv_sem=a_recv.at[g],
            device_id=(d, to),
            device_id_type=MESH,
        )

    def rotate(slot):
        yy = slot_y(slot)
        for hh in range(NH):
            p_copy(slot, hh, yy, 1 - c).wait_recv()
        pair = [fac_all[pl.ds(pl.multiple_of(pid(hh, yy, 0) * sb, 2 * sb), 2 * sb), 0 : kw * (hh + 1)] for hh in range(NH)]
        totals = [None] * NH
        for t in range(NH):
            stacked = jnp.concatenate([pair[hh][:, t * kw : (t + 1) * kw] for hh in range(t, NH)], axis=0)
            high, low = split(stacked)
            product = nt_dot(jnp.concatenate([high, high, low], axis=1), fcat[t])
            for hh in range(t, NH):
                piece = product[(hh - t) * 2 * sb : (hh - t + 1) * 2 * sb]
                totals[hh] = piece if totals[hh] is None else totals[hh] + piece
        for hh in range(NH):
            for cc in range(2):
                rot[pid(hh, yy, cc)] = totals[hh][cc * sb : (cc + 1) * sb]
        for step in range(1, NH + 1):
            for cs in range(2):
                hh = lax.rem(h + step, NH)
                cc = lax.rem(c + 1 + cs, 2)
                if slot == 0 and step == NH and cs == 1:
                    moved[g] = rot[g]
                else:
                    a_copy(hh, yy, cc).start()

    lane = lax.broadcasted_iota(jnp.int32, kinds_hbm.shape[1:], 1)
    sub = lax.broadcasted_iota(jnp.int32, kinds_hbm.shape[1:], 0)
    py, pz = kinds_hbm.shape[1], kinds_hbm.shape[2]

    first_in = jnp.where(d == 0, DEEP, 0)
    first_out = jnp.where(d == doms - 1, planes + DEEP, planes + 2 * DEEP)

    def k_copy(up):
        size = pl.ds(planes if up else DEEP, DEEP)
        return pltpu.make_async_remote_copy(
            src_ref=kinds_ref.at[size],
            dst_ref=kinds_ref.at[pl.ds(0 if up else planes + DEEP, DEEP)],
            send_sem=k_send.at[0 if up else 1],
            recv_sem=k_recv.at[0 if up else 1],
            device_id=(d + 1 if up else d - 1, g),
            device_id_type=MESH,
        )

    @pl.when(d < doms - 1)
    def _():
        k_copy(True).start()

    @pl.when(d > 0)
    def _():
        k_copy(False).start()

    def coefficients(i, carry):
        inside = jnp.logical_and(i >= first_in, i < first_out)
        for dz in (-1, 0, 1):
            kr = kinds_ref[i]
            if dz != 0:
                kr = pltpu.roll(kr, dz % pz, 1)
            hits = [kr == j for j in range(table_ref.shape[0])]
            for dx in (-1, 0, 1):
                for dy in (-1, 0, 1):
                    o = (dx + 1) * 9 + (dy + 1) * 3 + dz + 1
                    value = jnp.zeros(kr.shape, F32)
                    for j in range(table_ref.shape[0]):
                        value = jnp.where(hits[j], 2.0 * table_ref[j, o], value)
                    if dz == 1:
                        value = jnp.where(lane == 0, 0.0, value)
                    if dz == -1:
                        value = jnp.where(lane == pz - 1, 0.0, value)
                    if dy == 1:
                        value = jnp.where(sub == py - 1, 0.0, value)
                    if dy == -1:
                        value = jnp.where(sub == 0, 0.0, value)
                    coef[i, o] = jnp.where(inside, value, 0.0)
        return carry

    def make_coefficients():
        @pl.when(d == 0)
        def _():
            kinds_ref[0:DEEP] = jnp.zeros((DEEP, py, pz), jnp.int32)

        @pl.when(d == doms - 1)
        def _():
            kinds_ref[planes + DEEP : planes + 2 * DEEP] = jnp.zeros((DEEP, py, pz), jnp.int32)

        @pl.when(d > 0)
        def _():
            k_copy(True).wait_recv()

        @pl.when(d < doms - 1)
        def _():
            k_copy(False).wait_recv()

        lax.fori_loop(0, planes + 2 * DEEP, coefficients, 0)

    def place(i, carry):
        hh = lax.rem(i, NH)
        slot = i // NH
        t = (slot + 1) // 2
        yy = wrap(jnp.where(lax.rem(slot, 2) == 1, y + t, y - t))
        a_parts, b_parts = [], []
        for cc in range(2):
            src = pid(hh, yy, cc)

            @pl.when(src != g)
            def _(src=src):
                pltpu.make_async_remote_copy(
                    src_ref=rot.at[src],
                    dst_ref=moved.at[src],
                    send_sem=a_send.at[src],
                    recv_sem=a_recv.at[src],
                    device_id=(d, src),
                    device_id_type=MESH,
                ).wait_recv()

            cell = jnp.concatenate([map_ref[pl.ds(2 * src + i, 1), :] for i in range(2)], axis=1)
            row = (cell // 2048) * 8 + lax.rem(cell // 128, 8)
            column = lax.rem(cell // 1024, 2) * 128 + lax.rem(cell, 128)
            high, low = split(moved[src])
            row16 = jnp.broadcast_to(row.astype(F32), (sb, nb)).astype(BF16)
            for value in (high, low):
                a_parts.append(
                    jnp.concatenate([jnp.where(row16 == BF16(r), value, BF16(0)) for r in range(rows)], axis=0)
                )
            wide = jnp.broadcast_to(column, (256, nb))
            onehot = (wide == lax.broadcasted_iota(jnp.int32, (256, nb), 0)).astype(F32).astype(BF16)
            b_parts += [onehot, onehot]
        product = nt_dot(jnp.concatenate(a_parts, axis=1), jnp.concatenate(b_parts, axis=1))
        acc[0] += product[:, 0:128]
        acc[1] += product[:, 128:256]
        return carry

    rotate(0)
    make_coefficients()
    acc[...] = jnp.zeros_like(acc)
    placed = 0
    for t in range(1, half + 1):
        slots = [last] if t == half else [2 * t - 1, 2 * t]
        for hh in range(NH):
            for slot in slots:
                yy = slot_y(slot)
                y_copy(slot, hh, yy, right).wait_recv()
                if t < half - 1:
                    y_copy(slot + 2, hh, yy, right if slot % 2 == 1 else left).start()
                p_copy(slot, hh, yy, c).start()
            if t == half - 1:
                y_copy(last, hh, last_from, last_to).start()
        for slot in slots:
            rotate(slot)
        ready = max(2 * (t - LAG) + 1, 0)
        if ready > placed:
            lax.fori_loop(placed * NH, ready * NH, place, 0)
            placed = ready
    lax.fori_loop(placed * NH, ny * NH, place, 0)

    def lift(x):
        def one(s, carry):
            terms[0, x + CHEB, s] = acc[x % 2, pl.ds((x // 2) * py * sb + s, py, stride=sb), :]
            return carry

        lax.fori_loop(0, sb, one, 0, unroll=True)

    def halo(j, up):
        return pltpu.make_async_remote_copy(
            src_ref=terms.at[0, CHEB + planes - j if up else CHEB + j - 1],
            dst_ref=terms.at[0, CHEB - j if up else CHEB + planes + j - 1],
            send_sem=h_send.at[j - 1, 0 if up else 1],
            recv_sem=h_recv.at[j - 1, 0 if up else 1],
            device_id=(d + 1 if up else d - 1, g),
            device_id_type=MESH,
        )

    @pl.when(d == 0)
    def _():
        terms[0, 0:CHEB] = jnp.zeros((CHEB,) + terms.shape[2:], F32)

    @pl.when(d == doms - 1)
    def _():
        terms[0, planes + CHEB : planes + 2 * CHEB] = jnp.zeros((CHEB,) + terms.shape[2:], F32)

    lifted = []
    for j in range(1, CHEB + 1):
        for x in (planes - j, j - 1):
            if x not in lifted:
                lift(x)
                lifted.append(x)

        @pl.when(d < doms - 1)
        def _(j=j):
            halo(j, True).start()

        @pl.when(d > 0)
        def _(j=j):
            halo(j, False).start()

    for x in range(planes):
        if x not in lifted:
            lift(x)

    def plane(k, x):
        for first in range(0, sb, 4):
            block = slice(first, first + 4)
            sums = [None, None, None]
            for dx in range(3):
                mid = terms[k, x + CHEB - 1 + dx, block]
                shifted = (pltpu.roll(mid, 1, 1), mid, pltpu.roll(mid, py - 1, 1))
                for dy in range(3):
                    for dz in range(3):
                        term = coef[x + DEEP, dx * 9 + dy * 3 + dz][None] * shifted[dy]
                        sums[dz] = term if sums[dz] is None else sums[dz] + term
            total = sums[1] + pltpu.roll(sums[0], 1, 2) + pltpu.roll(sums[2], pz - 1, 2)
            if k == 0:
                total = 0.5 * total
            else:
                total = total - terms[k - 1, x + CHEB, block]
            if k == CHEB - 1:
                out_ref[block, x] = total
            else:
                terms[k + 1, x + CHEB, block] = total

    for k in range(CHEB):

        def interior(x, carry, k=k):
            plane(k, x)
            return carry

        lax.fori_loop(k + 1, planes - 1 - k, interior, 0)
    for j in range(1, CHEB + 1):

        @pl.when(d > 0)
        def _(j=j):
            halo(j, True).wait_recv()

        @pl.when(d < doms - 1)
        def _(j=j):
            halo(j, False).wait_recv()

        for k in range(CHEB):
            low, high = k + 1 - j, planes - 2 - k + j

            def both(i, carry, k=k, low=low, high=high):
                plane(k, low + i * (high - low))
                return carry

            lax.fori_loop(0, 2, both, 0)

    for step in range(1, NH):
        for hs in range(NH):

            @pl.when(h == hs)
            def _(hs=hs, step=step):
                z_copy(hs, step).wait_send()

    for slot in range(1, 2 * half):
        for hh in range(NH):
            y_copy(slot, hh, y, right).wait_send()
    for slot in range(2 * half):
        for hh in range(NH):
            p_copy(slot, hh, y, c).wait_send()

    def sent(i, carry):
        to = lax.rem(g + i, peers)
        pltpu.make_async_remote_copy(
            src_ref=rot.at[to],
            dst_ref=moved.at[g],
            send_sem=a_send.at[to],
            recv_sem=a_recv.at[g],
            device_id=(d, to),
            device_id_type=MESH,
        ).wait_send()
        return carry

    lax.fori_loop(1, peers, sent, 0)
    @pl.when(d < doms - 1)
    def _():
        k_copy(True).wait_send()
        for j in range(1, CHEB + 1):
            halo(j, True).wait_send()

    @pl.when(d > 0)
    def _():
        k_copy(False).wait_send()
        for j in range(1, CHEB + 1):
            halo(j, False).wait_send()


def local(doms, peers, features, factor, slab_map, kinds, kind_table):
    nb, states = features.shape
    sb = factor.shape[1]
    ny = peers // (2 * NH)
    planes, py, pz = kinds.shape
    cells = slab_map.shape[0]
    dma = pltpu.SemaphoreType.DMA
    vmem = pl.BlockSpec(memory_space=pltpu.VMEM)
    return pl.pallas_call(
        functools.partial(kernel, doms, ny),
        out_shape=jax.ShapeDtypeStruct((sb, planes, py, pz), F32),
        in_specs=[pl.BlockSpec(memory_space=pltpu.HBM)] * 4 + [pl.BlockSpec(memory_space=pltpu.SMEM)],
        out_specs=vmem,
        scratch_shapes=[
            pltpu.VMEM((nb, states), F32),
            pltpu.VMEM((cells // 128, 128), jnp.int32),
            pltpu.VMEM((planes + 2 * DEEP, py, pz), jnp.int32),
            pltpu.VMEM((states, states), F32),
            pltpu.VMEM((NH, nb, states), BF16),
            pltpu.VMEM((peers, sb, nb), F32),
            pltpu.VMEM((peers, sb, nb), F32),
            pltpu.VMEM((2, cells // 256 * sb, 128), F32),
            pltpu.VMEM((planes + 2 * DEEP, 27, py, pz), F32),
            pltpu.VMEM((CHEB, planes + 2 * CHEB, sb, py, pz), F32),
            dma((NH - 1,)),
            dma((NH,)),
            dma((ny, NH)),
            dma((ny, NH)),
            dma((ny, NH)),
            dma((ny, NH)),
            dma((peers,)),
            dma((peers,)),
            dma((CHEB, 2)),
            dma((CHEB, 2)),
            dma((2,)),
            dma((2,)),
            dma((4,)),
        ],
        compiler_params=pltpu.CompilerParams(
            collective_id=0, has_side_effects=True, vmem_limit_bytes=63 * 1024 * 1024
        ),
    )(features, factor.T, slab_map.reshape(cells // 128, 128), kinds, kind_table)


def solution(mesh):
    return jax.shard_map(
        functools.partial(local, mesh.shape["dom"], mesh.shape["grp"]),
        mesh=mesh,
        in_specs=(P(("dom", "grp"), None), P(None, "grp"), P("dom"), P("dom", None, None), P()),
        out_specs=P("grp", "dom", None, None),
        check_vma=False,
    )
```

```python
import functools

import jax
import jax.numpy as jnp
from jax import lax
from jax.experimental import pallas as pl
from jax.experimental.pallas import tpu as pltpu
from jax.sharding import PartitionSpec as P

CHEB = 4
NH = 3
DEEP = CHEB - 1
LAG = 1
MESH = pl.DeviceIdType.MESH
F32 = jnp.float32
BF16 = jnp.bfloat16


def split(value):
    high = value.astype(BF16)
    low = (value - high.astype(F32)).astype(BF16)
    return high, low


def nt_dot(a, b):
    return lax.dot_general(a, b, (((1,), (1,)), ((), ())), preferred_element_type=F32)


def kernel(
    doms,
    ny,
    feat_hbm,
    fac_hbm,
    map_hbm,
    kinds_hbm,
    table_ref,
    out_ref,
    feat_ref,
    map_ref,
    kinds_ref,
    fac_all,
    fcat,
    rot,
    moved,
    acc,
    coef,
    terms,
    z_send,
    z_recv,
    y_send,
    y_recv,
    p_send,
    p_recv,
    a_send,
    a_recv,
    h_send,
    h_recv,
    k_send,
    k_recv,
    fetched,
):
    peers = NH * ny * 2
    half = ny // 2
    sb, states = fac_hbm.shape
    nb = feat_hbm.shape[0]
    kw = states // NH
    planes = kinds_hbm.shape[0]
    rows = map_hbm.shape[0] * map_hbm.shape[1] // 256

    d = lax.axis_index("dom")
    g = lax.axis_index("grp")
    h = g // (2 * ny)
    y = lax.rem(g // 2, ny)
    c = lax.rem(g, 2)

    def pid(hh, yy, cc):
        return (hh * ny + yy) * 2 + cc

    def wrap(yy):
        return lax.rem(yy + 2 * ny, ny)

    own_rows = pl.ds(pl.multiple_of(g * sb, sb), sb)
    fetches = [
        pltpu.make_async_copy(fac_hbm, fac_all.at[own_rows], fetched.at[0]),
        pltpu.make_async_copy(feat_hbm, feat_ref, fetched.at[1]),
        pltpu.make_async_copy(kinds_hbm, kinds_ref.at[pl.ds(DEEP, planes)], fetched.at[2]),
        pltpu.make_async_copy(map_hbm, map_ref, fetched.at[3]),
    ]
    for fetch in fetches:
        fetch.start()

    barrier = pltpu.get_barrier_semaphore()
    near = [pid(h, wrap(y + 1), c), pid(h, wrap(y - 1), c), pid(h, y, 1 - c)]
    near += [pid(lax.rem(h + step, NH), y, c) for step in range(1, NH)]
    for to in near:
        pl.semaphore_signal(barrier, inc=1, device_id=(d, to), device_id_type=MESH)

    @pl.when(d > 0)
    def _():
        pl.semaphore_signal(barrier, inc=1, device_id=(d - 1, g), device_id_type=MESH)

    @pl.when(d < doms - 1)
    def _():
        pl.semaphore_signal(barrier, inc=1, device_id=(d + 1, g), device_id_type=MESH)

    for fetch in fetches:
        fetch.wait()
    f_high, f_low = split(feat_ref[...])
    for t in range(NH):
        part = slice(t * kw, (t + 1) * kw)
        fcat[t, :, 0:kw] = f_high[:, part]
        fcat[t, :, kw : 2 * kw] = f_low[:, part]
        fcat[t, :, 2 * kw : 3 * kw] = f_high[:, part]

    expected = len(near) + (d > 0).astype(jnp.int32) + (d < doms - 1).astype(jnp.int32)
    pl.semaphore_wait(barrier, expected)

    def block(hh, yy, cc):
        row = pl.multiple_of(pid(hh, yy, cc) * sb, sb)
        return fac_all.at[pl.ds(row, sb), pl.ds(0, kw * (hh + 1))]

    def z_copy(hs, step):
        to = lax.rem(h + step, NH)
        return pltpu.make_async_remote_copy(
            src_ref=block(hs, y, c),
            dst_ref=block(hs, y, c),
            send_sem=z_send.at[step - 1],
            recv_sem=z_recv.at[hs],
            device_id=(d, pid(to, y, c)),
            device_id_type=MESH,
        )

    def y_copy(slot, hh, from_y, to_y):
        return pltpu.make_async_remote_copy(
            src_ref=block(hh, from_y, c),
            dst_ref=block(hh, from_y, c),
            send_sem=y_send.at[slot, hh],
            recv_sem=y_recv.at[slot, hh],
            device_id=(d, pid(h, to_y, c)),
            device_id_type=MESH,
        )

    def p_copy(slot, hh, yy, cc):
        return pltpu.make_async_remote_copy(
            src_ref=block(hh, yy, cc),
            dst_ref=block(hh, yy, cc),
            send_sem=p_send.at[slot, hh],
            recv_sem=p_recv.at[slot, hh],
            device_id=(d, pid(h, y, 1 - c)),
            device_id_type=MESH,
        )

    right, left = wrap(y + 1), wrap(y - 1)
    last = 2 * half - 1
    last_from = wrap(jnp.where(c == 0, y - (half - 1), y + (half - 1)))
    last_to = jnp.where(c == 0, right, left)

    def slot_y(slot):
        if slot == 0:
            return y
        t = (slot + 1) // 2
        if slot == last:
            return wrap(y + half)
        return wrap(y - t) if slot % 2 == 1 else wrap(y + t)

    for hs in range(NH):

        @pl.when(h == hs)
        def _(hs=hs):
            for step in range(1, NH):
                z_copy(hs, step).start()
            y_copy(1, hs, y, right).start()
            if last != 1:
                y_copy(2, hs, y, left).start()
            p_copy(0, hs, y, c).start()

    for hs in range(NH):

        @pl.when(h != hs)
        def _(hs=hs):
            z_copy(hs, 1).wait_recv()
            y_copy(1, hs, y, right).start()
            if last != 1:
                y_copy(2, hs, y, left).start()
            p_copy(0, hs, y, c).start()

    def a_copy(hh, yy, cc):
        to = pid(hh, yy, cc)
        return pltpu.make_async_remote_copy(
            src_ref=rot.at[to],
            dst_ref=moved.at[g],
            send_sem=a_send.at[to],
            recv_sem=a_recv.at[g],
            device_id=(d, to),
            device_id_type=MESH,
        )

    def rotate(slot):
        yy = slot_y(slot)
        for hh in range(NH):
            p_copy(slot, hh, yy, 1 - c).wait_recv()
        pair = [fac_all[pl.ds(pl.multiple_of(pid(hh, yy, 0) * sb, 2 * sb), 2 * sb), 0 : kw * (hh + 1)] for hh in range(NH)]
        totals = [None] * NH
        for t in range(NH):
            stacked = jnp.concatenate([pair[hh][:, t * kw : (t + 1) * kw] for hh in range(t, NH)], axis=0)
            high, low = split(stacked)
            product = nt_dot(jnp.concatenate([high, high, low], axis=1), fcat[t])
            for hh in range(t, NH):
                piece = product[(hh - t) * 2 * sb : (hh - t + 1) * 2 * sb]
                totals[hh] = piece if totals[hh] is None else totals[hh] + piece
        for hh in range(NH):
            for cc in range(2):
                rot[pid(hh, yy, cc)] = totals[hh][cc * sb : (cc + 1) * sb]
        for step in range(1, NH + 1):
            for cs in range(2):
                hh = lax.rem(h + step, NH)
                cc = lax.rem(c + 1 + cs, 2)
                if slot == 0 and step == NH and cs == 1:
                    moved[g] = rot[g]
                else:
                    a_copy(hh, yy, cc).start()

    lane = lax.broadcasted_iota(jnp.int32, kinds_hbm.shape[1:], 1)
    sub = lax.broadcasted_iota(jnp.int32, kinds_hbm.shape[1:], 0)
    py, pz = kinds_hbm.shape[1], kinds_hbm.shape[2]

    first_in = jnp.where(d == 0, DEEP, 0)
    first_out = jnp.where(d == doms - 1, planes + DEEP, planes + 2 * DEEP)

    def k_copy(up):
        size = pl.ds(planes if up else DEEP, DEEP)
        return pltpu.make_async_remote_copy(
            src_ref=kinds_ref.at[size],
            dst_ref=kinds_ref.at[pl.ds(0 if up else planes + DEEP, DEEP)],
            send_sem=k_send.at[0 if up else 1],
            recv_sem=k_recv.at[0 if up else 1],
            device_id=(d + 1 if up else d - 1, g),
            device_id_type=MESH,
        )

    @pl.when(d < doms - 1)
    def _():
        k_copy(True).start()

    @pl.when(d > 0)
    def _():
        k_copy(False).start()

    def coefficients(i, carry):
        inside = jnp.logical_and(i >= first_in, i < first_out)
        for dz in (-1, 0, 1):
            kr = kinds_ref[i]
            if dz != 0:
                kr = pltpu.roll(kr, dz % pz, 1)
            hits = [kr == j for j in range(table_ref.shape[0])]
            for dx in (-1, 0, 1):
                for dy in (-1, 0, 1):
                    o = (dx + 1) * 9 + (dy + 1) * 3 + dz + 1
                    value = jnp.zeros(kr.shape, F32)
                    for j in range(table_ref.shape[0]):
                        value = jnp.where(hits[j], 2.0 * table_ref[j, o], value)
                    if dz == 1:
                        value = jnp.where(lane == 0, 0.0, value)
                    if dz == -1:
                        value = jnp.where(lane == pz - 1, 0.0, value)
                    if dy == 1:
                        value = jnp.where(sub == py - 1, 0.0, value)
                    if dy == -1:
                        value = jnp.where(sub == 0, 0.0, value)
                    coef[i, o] = jnp.where(inside, value, 0.0)
        return carry

    def make_coefficients():
        @pl.when(d == 0)
        def _():
            kinds_ref[0:DEEP] = jnp.zeros((DEEP, py, pz), jnp.int32)

        @pl.when(d == doms - 1)
        def _():
            kinds_ref[planes + DEEP : planes + 2 * DEEP] = jnp.zeros((DEEP, py, pz), jnp.int32)

        @pl.when(d > 0)
        def _():
            k_copy(True).wait_recv()

        @pl.when(d < doms - 1)
        def _():
            k_copy(False).wait_recv()

        lax.fori_loop(0, planes + 2 * DEEP, coefficients, 0)

    def place(i, carry):
        hh = lax.rem(i, NH)
        slot = i // NH
        t = (slot + 1) // 2
        yy = wrap(jnp.where(lax.rem(slot, 2) == 1, y + t, y - t))
        a_parts, b_parts = [], []
        for cc in range(2):
            src = pid(hh, yy, cc)

            @pl.when(src != g)
            def _(src=src):
                pltpu.make_async_remote_copy(
                    src_ref=rot.at[src],
                    dst_ref=moved.at[src],
                    send_sem=a_send.at[src],
                    recv_sem=a_recv.at[src],
                    device_id=(d, src),
                    device_id_type=MESH,
                ).wait_recv()

            cell = jnp.concatenate([map_ref[pl.ds(2 * src + i, 1), :] for i in range(2)], axis=1)
            row = (cell // 2048) * 8 + lax.rem(cell // 128, 8)
            column = lax.rem(cell // 1024, 2) * 128 + lax.rem(cell, 128)
            high, low = split(moved[src])
            row16 = jnp.broadcast_to(row.astype(F32), (sb, nb)).astype(BF16)
            for value in (high, low):
                a_parts.append(
                    jnp.concatenate([jnp.where(row16 == BF16(r), value, BF16(0)) for r in range(rows)], axis=0)
                )
            wide = jnp.broadcast_to(column, (256, nb))
            onehot = (wide == lax.broadcasted_iota(jnp.int32, (256, nb), 0)).astype(F32).astype(BF16)
            b_parts += [onehot, onehot]
        product = nt_dot(jnp.concatenate(a_parts, axis=1), jnp.concatenate(b_parts, axis=1))
        acc[0] += product[:, 0:128]
        acc[1] += product[:, 128:256]
        return carry

    rotate(0)
    make_coefficients()
    acc[...] = jnp.zeros_like(acc)
    placed = 0
    for t in range(1, half + 1):
        slots = [last] if t == half else [2 * t - 1, 2 * t]
        for hh in range(NH):
            for slot in slots:
                yy = slot_y(slot)
                y_copy(slot, hh, yy, right).wait_recv()
                if t < half - 1:
                    y_copy(slot + 2, hh, yy, right if slot % 2 == 1 else left).start()
                p_copy(slot, hh, yy, c).start()
            if t == half - 1:
                y_copy(last, hh, last_from, last_to).start()
        for slot in slots:
            rotate(slot)
        ready = max(2 * (t - LAG) + 1, 0)
        if ready > placed:
            lax.fori_loop(placed * NH, ready * NH, place, 0)
            placed = ready
    lax.fori_loop(placed * NH, ny * NH, place, 0)

    def lift(x):
        def one(s, carry):
            terms[0, x + CHEB, s] = acc[x % 2, pl.ds((x // 2) * py * sb + s, py, stride=sb), :]
            return carry

        lax.fori_loop(0, sb, one, 0, unroll=True)

    def halo(j, up):
        return pltpu.make_async_remote_copy(
            src_ref=terms.at[0, CHEB + planes - j if up else CHEB + j - 1],
            dst_ref=terms.at[0, CHEB - j if up else CHEB + planes + j - 1],
            send_sem=h_send.at[j - 1, 0 if up else 1],
            recv_sem=h_recv.at[j - 1, 0 if up else 1],
            device_id=(d + 1 if up else d - 1, g),
            device_id_type=MESH,
        )

    @pl.when(d == 0)
    def _():
        terms[0, 0:CHEB] = jnp.zeros((CHEB,) + terms.shape[2:], F32)

    @pl.when(d == doms - 1)
    def _():
        terms[0, planes + CHEB : planes + 2 * CHEB] = jnp.zeros((CHEB,) + terms.shape[2:], F32)

    lifted = []
    for j in range(1, CHEB + 1):
        for x in (planes - j, j - 1):
            if x not in lifted:
                lift(x)
                lifted.append(x)

        @pl.when(d < doms - 1)
        def _(j=j):
            halo(j, True).start()

        @pl.when(d > 0)
        def _(j=j):
            halo(j, False).start()

    for x in range(planes):
        if x not in lifted:
            lift(x)

    def plane(k, x):
        for first in range(0, sb, 4):
            block = slice(first, first + 4)
            sums = [None, None, None]
            for dx in range(3):
                mid = terms[k, x + CHEB - 1 + dx, block]
                shifted = (pltpu.roll(mid, 1, 1), mid, pltpu.roll(mid, py - 1, 1))
                for dy in range(3):
                    for dz in range(3):
                        term = coef[x + DEEP, dx * 9 + dy * 3 + dz][None] * shifted[dy]
                        sums[dz] = term if sums[dz] is None else sums[dz] + term
            total = sums[1] + pltpu.roll(sums[0], 1, 2) + pltpu.roll(sums[2], pz - 1, 2)
            if k == 0:
                total = 0.5 * total
            else:
                total = total - terms[k - 1, x + CHEB, block]
            if k == CHEB - 1:
                out_ref[block, x] = total
            else:
                terms[k + 1, x + CHEB, block] = total

    for k in range(CHEB):

        def interior(x, carry, k=k):
            plane(k, x)
            return carry

        lax.fori_loop(k + 1, planes - 1 - k, interior, 0)
    for j in range(1, CHEB + 1):

        @pl.when(d > 0)
        def _(j=j):
            halo(j, True).wait_recv()

        @pl.when(d < doms - 1)
        def _(j=j):
            halo(j, False).wait_recv()

        for k in range(CHEB):
            low, high = k + 1 - j, planes - 2 - k + j

            def both(i, carry, k=k, low=low, high=high):
                plane(k, low + i * (high - low))
                return carry

            lax.fori_loop(0, 2, both, 0)

    for step in range(1, NH):
        for hs in range(NH):

            @pl.when(h == hs)
            def _(hs=hs, step=step):
                z_copy(hs, step).wait_send()

    for slot in range(1, 2 * half):
        for hh in range(NH):
            y_copy(slot, hh, y, right).wait_send()
    for slot in range(2 * half):
        for hh in range(NH):
            p_copy(slot, hh, y, c).wait_send()

    def sent(i, carry):
        to = lax.rem(g + i, peers)
        pltpu.make_async_remote_copy(
            src_ref=rot.at[to],
            dst_ref=moved.at[g],
            send_sem=a_send.at[to],
            recv_sem=a_recv.at[g],
            device_id=(d, to),
            device_id_type=MESH,
        ).wait_send()
        return carry

    lax.fori_loop(1, peers, sent, 0)
    @pl.when(d < doms - 1)
    def _():
        k_copy(True).wait_send()
        for j in range(1, CHEB + 1):
            halo(j, True).wait_send()

    @pl.when(d > 0)
    def _():
        k_copy(False).wait_send()
        for j in range(1, CHEB + 1):
            halo(j, False).wait_send()


def local(doms, peers, features, factor, slab_map, kinds, kind_table):
    nb, states = features.shape
    sb = factor.shape[1]
    ny = peers // (2 * NH)
    planes, py, pz = kinds.shape
    cells = slab_map.shape[0]
    dma = pltpu.SemaphoreType.DMA
    vmem = pl.BlockSpec(memory_space=pltpu.VMEM)
    return pl.pallas_call(
        functools.partial(kernel, doms, ny),
        out_shape=jax.ShapeDtypeStruct((sb, planes, py, pz), F32),
        in_specs=[pl.BlockSpec(memory_space=pltpu.HBM)] * 4 + [pl.BlockSpec(memory_space=pltpu.SMEM)],
        out_specs=vmem,
        scratch_shapes=[
            pltpu.VMEM((nb, states), F32),
            pltpu.VMEM((cells // 128, 128), jnp.int32),
            pltpu.VMEM((planes + 2 * DEEP, py, pz), jnp.int32),
            pltpu.VMEM((states, states), F32),
            pltpu.VMEM((NH, nb, states), BF16),
            pltpu.VMEM((peers, sb, nb), F32),
            pltpu.VMEM((peers, sb, nb), F32),
            pltpu.VMEM((2, cells // 256 * sb, 128), F32),
            pltpu.VMEM((planes + 2 * DEEP, 27, py, pz), F32),
            pltpu.VMEM((CHEB, planes + 2 * CHEB, sb, py, pz), F32),
            dma((NH - 1,)),
            dma((NH,)),
            dma((ny, NH)),
            dma((ny, NH)),
            dma((ny, NH)),
            dma((ny, NH)),
            dma((peers,)),
            dma((peers,)),
            dma((CHEB, 2)),
            dma((CHEB, 2)),
            dma((2,)),
            dma((2,)),
            dma((4,)),
        ],
        compiler_params=pltpu.CompilerParams(
            collective_id=0, has_side_effects=True, vmem_limit_bytes=63 * 1024 * 1024
        ),
    )(features, factor.T, slab_map.reshape(cells // 128, 128), kinds, kind_table)


def solution(mesh):
    return jax.shard_map(
        functools.partial(local, mesh.shape["dom"], mesh.shape["grp"]),
        mesh=mesh,
        in_specs=(P(("dom", "grp"), None), P(None, "grp"), P("dom"), P("dom", None, None), P()),
        out_specs=P("grp", "dom", None, None),
        check_vma=False,
    )
```
